256 devices in a mesh: samp: 16 (over z, y_lo), par: 16 (over y_hi, x, core).
Axes of the slice: x: 4, y: 4 (y_hi: 2, y_lo: 2; y = y_hi * 2 + y_lo), z: 8, core: 2. Of those that a mesh axis runs over, the one named last changes fastest.
Arguments:
- jacobian: bfloat16 [16384, 8192], P('samp', 'par')
- partners: int32 [2, 16], replicated, may hold values from 0 to 15, as said below
Outputs:
- diag_tiles: float32 [16384, 1024], P(('samp', 'par'))
- cross_tiles: float32 [2, 16384, 1024], P(None, ('samp', 'par'))
The draws below stay inside these ranges and needn't reach their ends.
Inputs may be any that keep to these rules, and one draw needn't show every extreme that they name: partners[r, i] = i XOR m_r with a mask m_r taken from the seed; m_0 is neither 0 nor 16 - 1, and m_1 = m_0 XOR (15).
All inputs are finite; a program needn't handle non-finite values.
Results may differ from the reference program's by a relative error of at most 0.004.
Values may be sent and summed in bfloat16 or wider, within the bound.
No kernel may reach another device: no remote copies, remote signals or barrier semaphores. Data moves between devices by JAX's collectives and lax.ppermute only.
A program may use at most 64 MiB of HBM per device.

```python
import math
import jax
import jax.numpy as jnp
from jax import lax

S_DEV = 1024
PARAMS = 8192
ROUNDS = 2
NBLK = 16
SAMPLES = 16384


def draw_jacobian(key, part):
    key = jax.random.fold_in(key, 7)
    key_base, key_rows, key_cols, key_mean = jax.random.split(key, 4)
    base = jax.random.normal(key_base, (SAMPLES, PARAMS), jnp.float32)
    mean_scale = 0.5
    row_scale = jnp.exp(jax.random.uniform(key_rows, (SAMPLES, 1), jnp.float32, math.log(0.4), math.log(4.0)))
    col_scale = jnp.exp(jax.random.uniform(key_cols, (1, PARAMS), jnp.float32, math.log(0.4), math.log(4.0)))
    col_offset = mean_scale * jax.random.normal(key_mean, (1, PARAMS), jnp.float32)
    ramp_values = 1.0 + 2.0 * jnp.arange(SAMPLES, dtype=jnp.float32)[:, None] / SAMPLES
    values = (base * row_scale * col_scale + col_offset * ramp_values) * PARAMS ** (-0.4)
    return values.astype(jnp.bfloat16)


def draw_partners(key, part):
    key = jax.random.fold_in(key, 11)
    first_mask = jax.random.randint(key, (), 1, NBLK - 1, dtype=jnp.int32)
    masks = jnp.stack([first_mask, jnp.bitwise_xor(first_mask, NBLK - 1)])
    block_ids = jnp.arange(NBLK, dtype=jnp.int32)
    return jnp.bitwise_xor(block_ids[None, :], masks[:, None]).astype(jnp.int32)


def setup_inputs(seed: int = 0) -> dict:
    key_list = jax.random.split(jax.random.key(seed), 3)
    jacobian = draw_jacobian(jax.random.fold_in(key_list[2], 71), 0)
    partners = draw_partners(jax.random.fold_in(key_list[2], 71), 0)
    return dict(jacobian=jacobian, partners=partners)


def reference(jacobian, partners):
    col_mean = jnp.mean(jacobian.astype(jnp.float32), axis=0)
    centered = (jacobian.astype(jnp.float32) - col_mean).astype(jnp.bfloat16)
    stacked = centered.reshape(NBLK, S_DEV, PARAMS)

    def diagonal_tile(block_rows):
        return jnp.dot(block_rows, block_rows.T, preferred_element_type=jnp.float32)

    diag_tiles = lax.map(diagonal_tile, stacked).reshape(SAMPLES, S_DEV)

    def pair_tile(pair_args):
        block_rows, partner_index = pair_args
        partner_rows = stacked[partner_index]
        return jnp.dot(block_rows, partner_rows.T, preferred_element_type=jnp.float32)

    rounds_list = []
    for round_index in range(ROUNDS):
        tiles = lax.map(pair_tile, (stacked, partners[round_index].astype(jnp.int32)))
        rounds_list.append(tiles.reshape(SAMPLES, S_DEV))
    return diag_tiles, jnp.stack(rounds_list)
```

```python
import functools

import jax
import jax.numpy as jnp
import numpy as np
from jax import lax
from jax.sharding import Mesh, PartitionSpec as P

SAMP = ("z", "y_lo")
PAR = ("y_hi", "x", "core")
CHIPS = ("y_hi", "x")
CHUNKS = 2
BITS = {1: (0, 1), 2: (1, 3), 3: (1, 3), 4: (2, 1), 5: (2, 1), 6: (1, 3), 7: (2, 3)}


def parity(block, mask):
    s, t = BITS[mask]
    return ((block >> s) ^ (block >> t)) & 1


def sources(mask):
    return [i ^ (mask ^ 15 if parity(i, mask) else mask) for i in range(16)]


def gram(a, b):
    return lax.dot_general(a, b, (((1,), (1,)), ((), ())), preferred_element_type=jnp.float32)


def reduce_rows(partial):
    got = lax.all_to_all(partial.astype(jnp.bfloat16), CHIPS, 0, 0, tiled=True)
    return jnp.sum(got.astype(jnp.float32), axis=0)


def pick(halves, core):
    return jnp.where(core == 0, halves[:, 0], halves[:, 1])


def branch(mask, jac):
    core = lax.axis_index("core")
    src = sources(mask)
    same = [(s * 2 + c, d * 2 + c) for d, s in enumerate(src) for c in range(2)]
    other = [(s * 2 + c, d * 2 + 1 - c) for d, s in enumerate(src) for c in range(2)]
    back = [(d, s) for d, s in enumerate(src)]

    rows = jac.reshape(8, 2, CHUNKS, 64 // CHUNKS, 512)
    mine, theirs = pick(rows, core), pick(rows, 1 - core)
    raw = []
    for k in range(CHUNKS):
        a = lax.ppermute(mine[:, k].reshape(-1, 512), SAMP + ("core",), same)
        b = lax.ppermute(theirs[:, k].reshape(-1, 512), SAMP + ("core",), other)
        raw.append((a, b))

    sister = lax.ppermute(jac, "core", [(0, 1), (1, 0)])
    slab = jnp.concatenate([jac, sister], axis=1)
    col_total = jnp.sum(slab, axis=0, dtype=jnp.float32)
    totals = lax.all_to_all(jnp.broadcast_to(col_total, (16, 1024)), SAMP, 0, 0, tiled=True)
    col_mean = jnp.sum(totals, axis=0) / 16384

    def centre(x):
        return (x.astype(jnp.float32) - col_mean).astype(jnp.bfloat16)

    own = centre(slab)
    own_half = pick(own.reshape(8, 2, 64, 1024), core).reshape(512, 1024)
    diag = reduce_rows(gram(own_half, own).reshape(8, 64, 1024))

    parts = []
    for a, b in raw:
        partner = centre(jnp.concatenate([a, b], axis=1))
        parts.append(reduce_rows(gram(partner, own).reshape(8, 64 // CHUNKS, 1024)))
    result = jnp.concatenate(parts, axis=0).astype(jnp.bfloat16)

    arrived = lax.ppermute(result, SAMP, back).astype(jnp.float32)
    turned = lax.all_to_all(result.T.reshape(16, 64, 64), PAR, 0, 0, tiled=True)
    turned = turned.transpose(1, 0, 2).reshape(64, 1024).astype(jnp.float32)
    block = lax.axis_index(SAMP)
    return diag, turned, arrived, parity(block, mask)


def shards(jac, partners):
    first = partners[0, 0]
    flip = (first > 7).astype(jnp.int32)
    mask = jnp.minimum(first, 15 - first)
    branches = [functools.partial(branch, m) for m in range(1, 8)]
    diag, turned, arrived, par = lax.switch(mask - 1, branches, jac)
    cross = jnp.where((par ^ flip) == 0, jnp.stack([turned, arrived]), jnp.stack([arrived, turned]))
    return diag, cross


def solution(mesh):
    fine = Mesh(mesh.devices.reshape(8, 2, 2, 4, 2), SAMP + PAR)
    return jax.shard_map(
        shards,
        mesh=fine,
        in_specs=(P(SAMP, PAR), P()),
        out_specs=(P(SAMP + PAR, None), P(None, SAMP + PAR, None)),
        check_vma=False,
    )
```

```python
import functools

import jax
import jax.numpy as jnp
from jax import lax
from jax.experimental import pallas as pl
from jax.experimental.pallas import tpu as pltpu
from jax.sharding import Mesh, PartitionSpec as P

SAMP = ("z", "y_lo")
PAR = ("y_hi", "x", "core")
CHIPS = ("y_hi", "x")
BITS = {1: (0, 1), 2: (1, 3), 3: (1, 3), 4: (2, 1), 5: (2, 1), 6: (1, 3), 7: (2, 3)}
TILE = 256


def parity(block, mask):
    s, t = BITS[mask]
    return ((block >> s) ^ (block >> t)) & 1


def sources(mask):
    return [i ^ (mask ^ 15 if parity(i, mask) else mask) for i in range(16)]


def gram(a, b):
    return lax.dot_general(a, b, (((1,), (1,)), ((), ())), preferred_element_type=jnp.float32)


def centre(x, mean):
    return (x.astype(jnp.float32) - mean).astype(jnp.bfloat16)


def vmem_call(kernel, outs, scratch, flops):
    return pl.pallas_call(
        kernel,
        out_shape=outs,
        scratch_shapes=scratch,
        cost_estimate=pl.CostEstimate(flops=flops, bytes_accessed=6 << 20, transcendentals=0),
        compiler_params=pltpu.CompilerParams(vmem_limit_bytes=24 << 20),
    )


def total_kernel(own_ref, sister_ref, out_ref):
    ones = jnp.ones((16, 1024), jnp.bfloat16)
    out_ref[:, :512] = jnp.dot(ones, own_ref[...], preferred_element_type=jnp.float32)
    out_ref[:, 512:] = jnp.dot(ones, sister_ref[...], preferred_element_type=jnp.float32)


def column_mean(totals_ref):
    return jnp.sum(totals_ref[...], axis=0, keepdims=True) * (1.0 / 16384)


def product(rows_ref, own_ref, out_ref):
    @pl.loop(0, 1024 // TILE)
    def _(n):
        at = pl.ds(pl.multiple_of(n * TILE, TILE), TILE)
        out_ref[:, at] = gram(rows_ref[...], own_ref[at, :]).astype(jnp.bfloat16)


def own_kernel(own_ref, sister_ref, totals_ref, core_ref, centred_ref, out_ref, rows):
    mean = column_mean(totals_ref)
    core = core_ref[0]

    @pl.loop(0, 8)
    def _(c):
        at = pl.ds(pl.multiple_of(c * 128, 128), 128)
        centred_ref[at, :512] = centre(own_ref[at, :], mean[:, :512])
        centred_ref[at, 512:] = centre(sister_ref[at, :], mean[:, 512:])
        half = pl.ds(pl.multiple_of(c * 128 + core * 64, 64), 64)
        rows[pl.ds(pl.multiple_of(c * 64, 64), 64), :] = centred_ref[half, :]

    product(rows, centred_ref, out_ref)


def cross_kernel(raw_ref, totals_ref, centred_ref, out_ref, rows):
    mean = column_mean(totals_ref)

    @pl.loop(0, 8)
    def _(c):
        at = pl.ds(pl.multiple_of(c * 64, 64), 64)
        rows[at, :] = centre(raw_ref[at, :], mean)

    product(rows, centred_ref, out_ref)


def exchange(mask, half, jac, sister, totals, core):
    raw = lax.ppermute(half, SAMP, [(s, d) for d, s in enumerate(sources(mask))])
    own, partial = pl.pallas_call(
        own_kernel,
        out_shape=(
            jax.ShapeDtypeStruct((1024, 1024), jnp.bfloat16),
            jax.ShapeDtypeStruct((512, 1024), jnp.bfloat16),
        ),
        in_specs=[pl.BlockSpec(memory_space=pltpu.VMEM)] * 3 + [pl.BlockSpec(memory_space=pltpu.SMEM)],
        scratch_shapes=[pltpu.VMEM((512, 1024), jnp.bfloat16)],
        cost_estimate=pl.CostEstimate(flops=2 << 29, bytes_accessed=6 << 20, transcendentals=0),
        compiler_params=pltpu.CompilerParams(vmem_limit_bytes=24 << 20),
    )(jac, sister, totals, core)
    diag = lax.all_to_all(partial.reshape(8, 64, 1024), CHIPS, 0, 0, tiled=True)
    return raw, own, diag


def finish(mask, result, tiles):
    back = [(d, s) for d, s in enumerate(sources(mask))]
    arrived = lax.ppermute(result, SAMP, back)
    turned = lax.all_to_all(tiles, PAR, 0, 0, tiled=True)
    return arrived, turned, parity(lax.axis_index(SAMP), mask)


def shards(jac, partners):
    first = partners[0, 0]
    mask = jnp.minimum(first, 15 - first)
    core = lax.axis_index("core")
    sister = lax.ppermute(jac, "core", [(0, 1), (1, 0)])
    total = vmem_call(total_kernel, jax.ShapeDtypeStruct((16, 1024), jnp.float32), [], 2 * 16 << 20)(jac, sister)
    totals = lax.all_to_all(total, SAMP, 0, 0, tiled=True)
    slab = jnp.concatenate([jac, sister], axis=1).reshape(8, 2, 64, 1024)
    half = jnp.where(core == 0, slab[:, 0], slab[:, 1]).reshape(512, 1024)
    half, totals = lax.optimization_barrier((half, totals))
    raw, own, diag = lax.switch(
        mask - 1,
        [functools.partial(exchange, m) for m in range(1, 8)],
        half, jac, sister, totals, core.reshape(1),
    )
    diag = lax.optimization_barrier(diag)
    partial = vmem_call(
        cross_kernel,
        jax.ShapeDtypeStruct((512, 1024), jnp.bfloat16),
        [pltpu.VMEM((512, 1024), jnp.bfloat16)],
        2 << 29,
    )(raw, totals, own)
    got = lax.all_to_all(partial.reshape(8, 64, 1024), CHIPS, 0, 0, tiled=True)
    result = jnp.sum(got.astype(jnp.float32), axis=0).astype(jnp.bfloat16)
    arrived, turned, par = lax.switch(
        mask - 1, [functools.partial(finish, m) for m in range(1, 8)], result, result.T.reshape(16, 64, 64)
    )
    turned = turned.transpose(1, 0, 2).reshape(64, 1024)
    flip = (first > 7).astype(jnp.int32)
    cross = jnp.where((par ^ flip) == 0, jnp.stack([turned, arrived]), jnp.stack([arrived, turned]))
    return jnp.sum(diag.astype(jnp.float32), axis=0), cross.astype(jnp.float32)


def solution(mesh):
    fine = Mesh(mesh.devices.reshape(8, 2, 2, 4, 2), SAMP + PAR)
    return jax.shard_map(
        shards,
        mesh=fine,
        in_specs=(P(SAMP, PAR), P()),
        out_specs=(P(SAMP + PAR, None), P(None, SAMP + PAR, None)),
        check_vma=False,
    )
```

```python
import functools

import jax
import jax.numpy as jnp
from jax import lax
from jax.experimental import pallas as pl
from jax.experimental.pallas import tpu as pltpu
from jax.sharding import Mesh, PartitionSpec as P

SAMP = ("z", "y_lo")
PAR = ("y_hi", "x", "core")
CHIPS = ("y_hi", "x")
BITS = {1: (0, 1), 2: (1, 3), 3: (1, 3), 4: (2, 1), 5: (2, 1), 6: (1, 3), 7: (2, 3)}
TILE = 256


def parity(block, mask):
    s, t = BITS[mask]
    return ((block >> s) ^ (block >> t)) & 1


def sources(mask):
    return [i ^ (mask ^ 15 if parity(i, mask) else mask) for i in range(16)]


def gram(a, b):
    return lax.dot_general(a, b, (((1,), (1,)), ((), ())), preferred_element_type=jnp.float32)


def centre(x, mean):
    return (x.astype(jnp.float32) - mean).astype(jnp.bfloat16)


def vmem_call(kernel, outs, scratch, flops):
    return pl.pallas_call(
        kernel,
        out_shape=outs,
        scratch_shapes=scratch,
        cost_estimate=pl.CostEstimate(flops=flops, bytes_accessed=6 << 20, transcendentals=0),
        compiler_params=pltpu.CompilerParams(vmem_limit_bytes=24 << 20),
    )


def add_totals(ref, side, total_ref):
    ones = jnp.ones((16, 1024), jnp.bfloat16)
    total = jnp.dot(ones, ref[...], preferred_element_type=jnp.float32)
    for r in range(4):
        total_ref[:, side * 4 + r, :] = total[:, r * 128 : (r + 1) * 128]


def own_total_kernel(own_ref, total_ref):
    total_ref[...] = jnp.zeros_like(total_ref)
    add_totals(own_ref, 0, total_ref)


def sister_total_kernel(sister_ref, before_ref, total_ref):
    total_ref[...] = before_ref[...]
    add_totals(sister_ref, 1, total_ref)


def half_kernel(own_ref, sister_ref, core_ref, half_ref):
    core = core_ref[0]

    @pl.loop(0, 8)
    def _(c):
        at = pl.ds(pl.multiple_of(c * 64, 64), 64)
        half = pl.ds(pl.multiple_of(c * 128 + core * 64, 64), 64)
        half_ref[at, :512] = own_ref[half, :]
        half_ref[at, 512:] = sister_ref[half, :]


def column_mean(totals_ref):
    mean = jnp.sum(totals_ref[...], axis=0) * (1.0 / 16384)
    return jnp.concatenate([mean[r : r + 1] for r in range(8)], axis=1)


def own_kernel(own_ref, sister_ref, totals_ref, core_ref, centred_ref, out_ref, rows):
    mean = column_mean(totals_ref)
    core = core_ref[0]

    @pl.loop(0, 8)
    def _(c):
        at = pl.ds(pl.multiple_of(c * 128, 128), 128)
        centred_ref[at, :512] = centre(own_ref[at, :], mean[:, :512])
        centred_ref[at, 512:] = centre(sister_ref[at, :], mean[:, 512:])
        half = pl.ds(pl.multiple_of(c * 128 + core * 64, 64), 64)
        rows[pl.ds(pl.multiple_of(c * 64, 64), 64), :] = centred_ref[half, :]

    @pl.loop(0, 1024 // TILE)
    def _(n):
        at = pl.ds(pl.multiple_of(n * TILE, TILE), TILE)
        out_ref[:, at] = gram(rows[...], centred_ref[at, :]).astype(jnp.bfloat16)


def cross_kernel(raw_ref, totals_ref, centred_ref, out_ref, raw, rows, out, in_sem, out_sem):
    arrive = pltpu.make_async_copy(raw_ref, raw, in_sem)
    arrive.start()
    mean = column_mean(totals_ref)
    arrive.wait()
    rows[...] = centre(raw[...], mean)
    leave = []
    for n in range(1024 // TILE):
        at = pl.ds(n * TILE, TILE)
        out[:, at] = gram(rows[...], centred_ref[at, :]).astype(jnp.bfloat16)
        leave.append(pltpu.make_async_copy(out.at[:, at], out_ref.at[:, at], out_sem.at[n]))
        leave[-1].start()
    for copy in leave:
        copy.wait()


def fold_kernel(got_ref, result_ref, tiles_ref):
    total = jnp.sum(got_ref[...].astype(jnp.float32), axis=0)
    result_ref[...] = total.astype(jnp.bfloat16)
    for b in range(8):
        turned = total[:, b * 128 : (b + 1) * 128].T
        for p in range(2):
            tile = turned[p * 64 : (p + 1) * 64]
            tiles_ref[2 * b + p] = jnp.concatenate([tile[:32], tile[32:]], axis=1).astype(jnp.bfloat16)


def output_kernel(arrived_ref, tiles_ref, place_ref, out_ref):
    place = place_ref[0]
    out_ref[1 - place] = arrived_ref[...].astype(jnp.float32)
    for q in range(16):
        tile = tiles_ref[q].astype(jnp.float32)
        out_ref[place, :32, q * 64 : (q + 1) * 64] = tile[:, :64]
        out_ref[place, 32:, q * 64 : (q + 1) * 64] = tile[:, 64:]


def exchange(mask, total, jac, sister, core):
    totals = lax.all_to_all(total, SAMP, 0, 0, tiled=True)
    half = pl.pallas_call(
        half_kernel,
        out_shape=jax.ShapeDtypeStruct((512, 1024), jnp.bfloat16),
        in_specs=[pl.BlockSpec(memory_space=pltpu.VMEM)] * 2 + [pl.BlockSpec(memory_space=pltpu.SMEM)],
        cost_estimate=pl.CostEstimate(flops=0, bytes_accessed=2 << 20, transcendentals=0),
        compiler_params=pltpu.CompilerParams(vmem_limit_bytes=24 << 20),
    )(jac, sister, core)
    raw = lax.ppermute(half, SAMP, [(s, d) for d, s in enumerate(sources(mask))])
    own, partial = pl.pallas_call(
        own_kernel,
        out_shape=(
            jax.ShapeDtypeStruct((1024, 1024), jnp.bfloat16),
            jax.ShapeDtypeStruct((512, 1024), jnp.bfloat16),
        ),
        in_specs=[pl.BlockSpec(memory_space=pltpu.VMEM)] * 3 + [pl.BlockSpec(memory_space=pltpu.SMEM)],
        scratch_shapes=[pltpu.VMEM((512, 1024), jnp.bfloat16)],
        cost_estimate=pl.CostEstimate(flops=2 << 29, bytes_accessed=6 << 20, transcendentals=0),
        compiler_params=pltpu.CompilerParams(vmem_limit_bytes=24 << 20),
    )(jac, sister, totals, core)
    diag = lax.all_to_all(partial.reshape(8, 64, 1024), CHIPS, 0, 0, tiled=True)
    return raw, own, diag, totals


def finish(mask, result, tiles):
    back = [(d, s) for d, s in enumerate(sources(mask))]
    arrived = lax.ppermute(result, SAMP, back)
    turned = lax.all_to_all(tiles, PAR, 0, 0, tiled=True)
    return arrived, turned, parity(lax.axis_index(SAMP), mask)


def shards(jac, partners):
    first = partners[0, 0]
    mask = jnp.minimum(first, 15 - first)
    core = lax.axis_index("core")
    sister = lax.ppermute(jac, "core", [(0, 1), (1, 0)])
    sums = jax.ShapeDtypeStruct((16, 8, 128), jnp.float32)
    total = vmem_call(own_total_kernel, sums, [], 16 << 20)(jac)
    total = vmem_call(sister_total_kernel, sums, [], 16 << 20)(sister, total)
    raw, own, diag, totals = lax.switch(
        mask - 1,
        [functools.partial(exchange, m) for m in range(1, 8)],
        total, jac, sister, core.reshape(1),
    )
    diag = lax.optimization_barrier(diag)
    partial = pl.pallas_call(
        cross_kernel,
        out_shape=jax.ShapeDtypeStruct((512, 1024), jnp.bfloat16),
        in_specs=[pl.BlockSpec(memory_space=pl.ANY)] + [pl.BlockSpec(memory_space=pltpu.VMEM)] * 2,
        out_specs=pl.BlockSpec(memory_space=pl.ANY),
        scratch_shapes=[pltpu.VMEM((512, 1024), jnp.bfloat16)] * 3
        + [pltpu.SemaphoreType.DMA, pltpu.SemaphoreType.DMA((1024 // TILE,))],
        cost_estimate=pl.CostEstimate(flops=2 << 29, bytes_accessed=4 << 20, transcendentals=0),
        compiler_params=pltpu.CompilerParams(vmem_limit_bytes=24 << 20),
    )(raw, totals, own)
    got = lax.all_to_all(partial.reshape(8, 64, 1024), CHIPS, 0, 0, tiled=True)
    result, tiles = vmem_call(
        fold_kernel,
        (
            jax.ShapeDtypeStruct((64, 1024), jnp.bfloat16),
            jax.ShapeDtypeStruct((16, 32, 128), jnp.bfloat16),
        ),
        [],
        1 << 20,
    )(got)
    arrived, turned, par = lax.switch(
        mask - 1, [functools.partial(finish, m) for m in range(1, 8)], result, tiles
    )
    place = par ^ (first > 7).astype(jnp.int32)
    cross = pl.pallas_call(
        output_kernel,
        out_shape=jax.ShapeDtypeStruct((2, 64, 1024), jnp.float32),
        in_specs=[pl.BlockSpec(memory_space=pltpu.VMEM)] * 2 + [pl.BlockSpec(memory_space=pltpu.SMEM)],
        compiler_params=pltpu.CompilerParams(vmem_limit_bytes=24 << 20),
    )(arrived, turned, place.reshape(1))
    return jnp.sum(diag.astype(jnp.float32), axis=0), cross


def solution(mesh):
    fine = Mesh(mesh.devices.reshape(8, 2, 2, 4, 2), SAMP + PAR)
    return jax.shard_map(
        shards,
        mesh=fine,
        in_specs=(P(SAMP, PAR), P()),
        out_specs=(P(SAMP + PAR, None), P(None, SAMP + PAR, None)),
        check_vma=False,
    )
```

```python
import functools

import jax
import jax.numpy as jnp
from jax import lax
from jax.experimental import pallas as pl
from jax.experimental.pallas import tpu as pltpu
from jax.sharding import Mesh, PartitionSpec as P

SAMP = ("z", "y_lo")
PAR = ("y_hi", "x", "core")
CHIPS = ("y_hi", "x")
BITS = {1: (0, 1), 2: (1, 3), 3: (1, 3), 4: (2, 1), 5: (2, 1), 6: (1, 3), 7: (2, 3)}
TILE = 256


def parity(block, mask):
    s, t = BITS[mask]
    return ((block >> s) ^ (block >> t)) & 1


def sources(mask):
    return [i ^ (mask ^ 15 if parity(i, mask) else mask) for i in range(16)]


def gram(a, b):
    return lax.dot_general(a, b, (((1,), (1,)), ((), ())), preferred_element_type=jnp.float32)


def centre(x, mean):
    return (x.astype(jnp.float32) - mean).astype(jnp.bfloat16)


def vmem_call(kernel, outs, scratch, flops):
    return pl.pallas_call(
        kernel,
        out_shape=outs,
        scratch_shapes=scratch,
        cost_estimate=pl.CostEstimate(flops=flops, bytes_accessed=6 << 20, transcendentals=0),
        compiler_params=pltpu.CompilerParams(vmem_limit_bytes=24 << 20),
    )


def add_totals(ref, side, total_ref):
    ones = jnp.ones((16, 1024), jnp.bfloat16)
    total = jnp.dot(ones, ref[...], preferred_element_type=jnp.float32)
    for r in range(4):
        total_ref[:, side * 4 + r, :] = total[:, r * 128 : (r + 1) * 128]


def own_total_kernel(own_ref, partners_ref, total_ref, index_ref):
    first = partners_ref[0, 0]
    index_ref[0] = jnp.minimum(first, 15 - first) - 1
    total_ref[...] = jnp.zeros_like(total_ref)
    add_totals(own_ref, 0, total_ref)


def sister_total_kernel(sister_ref, before_ref, total_ref):
    total_ref[...] = before_ref[...]
    add_totals(sister_ref, 1, total_ref)


def half_kernel(own_ref, sister_ref, core_ref, half_ref):
    core = core_ref[0]

    @pl.loop(0, 8)
    def _(c):
        at = pl.ds(pl.multiple_of(c * 64, 64), 64)
        half = pl.ds(pl.multiple_of(c * 128 + core * 64, 64), 64)
        half_ref[at, :512] = own_ref[half, :]
        half_ref[at, 512:] = sister_ref[half, :]


def column_mean(totals_ref):
    mean = jnp.sum(totals_ref[...], axis=0) * (1.0 / 16384)
    return jnp.concatenate([mean[r : r + 1] for r in range(8)], axis=1)


def own_kernel(own_ref, sister_ref, totals_ref, core_ref, centred_ref, out_ref, rows):
    mean = column_mean(totals_ref)
    core = core_ref[0]

    @pl.loop(0, 8)
    def _(c):
        at = pl.ds(pl.multiple_of(c * 128, 128), 128)
        centred_ref[at, :512] = centre(own_ref[at, :], mean[:, :512])
        centred_ref[at, 512:] = centre(sister_ref[at, :], mean[:, 512:])
        half = pl.ds(pl.multiple_of(c * 128 + core * 64, 64), 64)
        put = pl.ds(pl.multiple_of(((c & 3) * 2 + (c >> 2)) * 64, 64), 64)
        rows[put, :] = centred_ref[half, :]

    @pl.loop(0, 1024 // TILE)
    def _(n):
        at = pl.ds(pl.multiple_of(n * TILE, TILE), TILE)
        out_ref[:, at] = gram(rows[...], centred_ref[at, :]).astype(jnp.bfloat16)


def cross_kernel(raw_ref, totals_ref, centred_ref, out_ref, raw, rows, out, in_sem, out_sem):
    arrive = pltpu.make_async_copy(raw_ref, raw, in_sem)
    arrive.start()
    mean = column_mean(totals_ref)
    arrive.wait()
    rows[...] = centre(raw[...], mean)
    leave = []
    for n in range(1024 // TILE):
        at = pl.ds(n * TILE, TILE)
        out[:, at] = gram(rows[...], centred_ref[at, :]).astype(jnp.bfloat16)
        leave.append(pltpu.make_async_copy(out.at[:, at], out_ref.at[:, at], out_sem.at[n]))
        leave[-1].start()
    for copy in leave:
        copy.wait()


def fold_kernel(got_ref, result_ref, tiles_ref):
    total = jnp.sum(got_ref[...].astype(jnp.float32), axis=0)
    result_ref[...] = total.astype(jnp.bfloat16)
    for b in range(8):
        turned = total[:, b * 128 : (b + 1) * 128].T
        for p in range(2):
            tile = turned[p * 64 : (p + 1) * 64]
            tiles_ref[2 * b + p] = jnp.concatenate([tile[:32], tile[32:]], axis=1).astype(jnp.bfloat16)


def output_kernel(arrived_ref, tiles_ref, keep_ref, other_ref, place_ref, diag_ref, out_ref):
    place = place_ref[0]
    diag_ref[...] = keep_ref[...] + other_ref[...].astype(jnp.float32)
    out_ref[1 - place] = arrived_ref[...].astype(jnp.float32)
    for q in range(16):
        tile = tiles_ref[q].astype(jnp.float32)
        out_ref[place, :32, q * 64 : (q + 1) * 64] = tile[:, :64]
        out_ref[place, 32:, q * 64 : (q + 1) * 64] = tile[:, 64:]


def exchange(mask, total, jac, sister, core):
    totals = lax.all_to_all(total, SAMP, 0, 0, tiled=True)
    half = pl.pallas_call(
        half_kernel,
        out_shape=jax.ShapeDtypeStruct((512, 1024), jnp.bfloat16),
        in_specs=[pl.BlockSpec(memory_space=pltpu.VMEM)] * 2 + [pl.BlockSpec(memory_space=pltpu.SMEM)],
        cost_estimate=pl.CostEstimate(flops=0, bytes_accessed=2 << 20, transcendentals=0),
        compiler_params=pltpu.CompilerParams(vmem_limit_bytes=24 << 20),
    )(jac, sister, core)
    raw = lax.ppermute(half, SAMP, [(s, d) for d, s in enumerate(sources(mask))])
    own, partial = pl.pallas_call(
        own_kernel,
        out_shape=(
            jax.ShapeDtypeStruct((1024, 1024), jnp.bfloat16),
            jax.ShapeDtypeStruct((512, 1024), jnp.bfloat16),
        ),
        in_specs=[pl.BlockSpec(memory_space=pltpu.VMEM)] * 3 + [pl.BlockSpec(memory_space=pltpu.SMEM)],
        scratch_shapes=[pltpu.VMEM((512, 1024), jnp.bfloat16)],
        cost_estimate=pl.CostEstimate(flops=2 << 31, bytes_accessed=6 << 20, transcendentals=0),
        compiler_params=pltpu.CompilerParams(vmem_limit_bytes=24 << 20),
    )(jac, sister, totals, core)
    diag = lax.all_to_all(partial.reshape(4, 128, 1024), "x", 0, 0, tiled=True)
    return raw, own, diag, totals


def finish(mask, result, tiles):
    back = [(d, s) for d, s in enumerate(sources(mask))]
    arrived = lax.ppermute(result, SAMP, back)
    turned = lax.all_to_all(tiles, PAR, 0, 0, tiled=True)
    return arrived, turned, parity(lax.axis_index(SAMP), mask)


def shards(jac, partners):
    first = partners[0, 0]
    core = lax.axis_index("core")
    sister = lax.ppermute(jac, "core", [(0, 1), (1, 0)])
    sums = jax.ShapeDtypeStruct((16, 8, 128), jnp.float32)
    total, index = pl.pallas_call(
        own_total_kernel,
        out_shape=(sums, jax.ShapeDtypeStruct((1,), jnp.int32)),
        in_specs=[pl.BlockSpec(memory_space=pltpu.VMEM), pl.BlockSpec(memory_space=pltpu.SMEM)],
        out_specs=(pl.BlockSpec(memory_space=pltpu.VMEM), pl.BlockSpec(memory_space=pltpu.SMEM)),
        cost_estimate=pl.CostEstimate(flops=16 << 20, bytes_accessed=1 << 20, transcendentals=0),
        compiler_params=pltpu.CompilerParams(vmem_limit_bytes=24 << 20),
    )(jac, partners)
    index = index[0]
    total = vmem_call(sister_total_kernel, sums, [], 16 << 20)(sister, total)
    raw, own, diag, totals = lax.switch(
        index,
        [functools.partial(exchange, m) for m in range(1, 8)],
        total, jac, sister, core.reshape(1),
    )
    diag = lax.optimization_barrier(diag)
    partial = pl.pallas_call(
        cross_kernel,
        out_shape=jax.ShapeDtypeStruct((512, 1024), jnp.bfloat16),
        in_specs=[pl.BlockSpec(memory_space=pl.ANY)] + [pl.BlockSpec(memory_space=pltpu.VMEM)] * 2,
        out_specs=pl.BlockSpec(memory_space=pl.ANY),
        scratch_shapes=[pltpu.VMEM((512, 1024), jnp.bfloat16)] * 3
        + [pltpu.SemaphoreType.DMA, pltpu.SemaphoreType.DMA((1024 // TILE,))],
        cost_estimate=pl.CostEstimate(flops=2 << 29, bytes_accessed=4 << 20, transcendentals=0),
        compiler_params=pltpu.CompilerParams(vmem_limit_bytes=24 << 20),
    )(raw, totals, own)
    diag = jnp.sum(diag.reshape(4, 2, 64, 1024).astype(jnp.float32), axis=0)
    y_hi = lax.axis_index("y_hi")
    keep, give = jnp.where(y_hi == 0, diag[0], diag[1]), jnp.where(y_hi == 0, diag[1], diag[0])
    other_half = lax.ppermute(give.astype(jnp.bfloat16), "y_hi", [(0, 1), (1, 0)])
    got = lax.all_to_all(partial.reshape(8, 64, 1024), CHIPS, 0, 0, tiled=True)
    result, tiles = vmem_call(
        fold_kernel,
        (
            jax.ShapeDtypeStruct((64, 1024), jnp.bfloat16),
            jax.ShapeDtypeStruct((16, 32, 128), jnp.bfloat16),
        ),
        [],
        1 << 20,
    )(got)
    arrived, turned, par = lax.switch(
        index, [functools.partial(finish, m) for m in range(1, 8)], result, tiles
    )
    place = par ^ (first > 7).astype(jnp.int32)
    return pl.pallas_call(
        output_kernel,
        out_shape=(
            jax.ShapeDtypeStruct((64, 1024), jnp.float32),
            jax.ShapeDtypeStruct((2, 64, 1024), jnp.float32),
        ),
        in_specs=[pl.BlockSpec(memory_space=pltpu.VMEM)] * 4 + [pl.BlockSpec(memory_space=pltpu.SMEM)],
        compiler_params=pltpu.CompilerParams(vmem_limit_bytes=24 << 20),
    )(arrived, turned, keep, other_half, place.reshape(1))


def solution(mesh):
    fine = Mesh(mesh.devices.reshape(8, 2, 2, 4, 2), SAMP + PAR)
    return jax.shard_map(
        shards,
        mesh=fine,
        in_specs=(P(SAMP, PAR), P()),
        out_specs=(P(SAMP + PAR, None), P(None, SAMP + PAR, None)),
        check_vma=False,
    )
```

```python
import functools

import jax
import jax.numpy as jnp
from jax import lax
from jax.experimental import pallas as pl
from jax.experimental.pallas import tpu as pltpu
from jax.sharding import Mesh, PartitionSpec as P

SAMP = ("z", "y_lo")
PAR = ("y_hi", "x", "core")
CHIPS = ("y_hi", "x")
BITS = {1: (0, 1), 2: (1, 3), 3: (1, 3), 4: (2, 1), 5: (2, 1), 6: (1, 3), 7: (2, 3)}
TILE = 256


def parity(block, mask):
    s, t = BITS[mask]
    return ((block >> s) ^ (block >> t)) & 1


def sources(mask):
    return [i ^ (mask ^ 15 if parity(i, mask) else mask) for i in range(16)]


def gram(a, b):
    return lax.dot_general(a, b, (((1,), (1,)), ((), ())), preferred_element_type=jnp.float32)


def centre(x, mean):
    return (x.astype(jnp.float32) - mean).astype(jnp.bfloat16)


def vmem_call(kernel, outs, scratch, flops):
    return pl.pallas_call(
        kernel,
        out_shape=outs,
        scratch_shapes=scratch,
        cost_estimate=pl.CostEstimate(flops=flops, bytes_accessed=6 << 20, transcendentals=0),
        compiler_params=pltpu.CompilerParams(vmem_limit_bytes=24 << 20),
    )


def add_totals(ref, side, total_ref):
    ones = jnp.ones((16, 1024), jnp.bfloat16)
    total = jnp.dot(ones, ref[...], preferred_element_type=jnp.float32)
    for r in range(4):
        total_ref[:, side * 4 + r, :] = total[:, r * 128 : (r + 1) * 128]


def own_total_kernel(own_ref, partners_ref, total_ref, index_ref):
    first = partners_ref[0, 0]
    index_ref[0] = jnp.minimum(first, 15 - first) - 1
    total_ref[...] = jnp.zeros_like(total_ref)
    add_totals(own_ref, 0, total_ref)


def sister_total_kernel(sister_ref, before_ref, total_ref):
    total_ref[...] = before_ref[...]
    add_totals(sister_ref, 1, total_ref)


def half_kernel(own_ref, sister_ref, core_ref, half_ref):
    core = core_ref[0]

    @pl.loop(0, 8)
    def _(c):
        at = pl.ds(pl.multiple_of(c * 64, 64), 64)
        half = pl.ds(pl.multiple_of(c * 128 + core * 64, 64), 64)
        half_ref[at, :512] = own_ref[half, :]
        half_ref[at, 512:] = sister_ref[half, :]


def column_mean(totals_ref):
    mean = jnp.sum(totals_ref[...], axis=0) * (1.0 / 16384)
    return jnp.concatenate([mean[r : r + 1] for r in range(8)], axis=1)


def own_kernel(own_ref, sister_ref, totals_ref, core_ref, centred_ref, out_ref, rows):
    mean = column_mean(totals_ref)
    core = core_ref[0]

    @pl.loop(0, 8)
    def _(c):
        at = pl.ds(pl.multiple_of(c * 128, 128), 128)
        centred_ref[at, :512] = centre(own_ref[at, :], mean[:, :512])
        centred_ref[at, 512:] = centre(sister_ref[at, :], mean[:, 512:])
        half = pl.ds(pl.multiple_of(c * 128 + core * 64, 64), 64)
        put = pl.ds(pl.multiple_of(((c & 3) * 2 + (c >> 2)) * 64, 64), 64)
        rows[put, :] = centred_ref[half, :]

    @pl.loop(0, 1024 // TILE)
    def _(n):
        at = pl.ds(pl.multiple_of(n * TILE, TILE), TILE)
        out_ref[:, at] = gram(rows[...], centred_ref[at, :]).astype(jnp.bfloat16)


def cross_kernel(raw_ref, totals_ref, centred_ref, out_ref, raw, rows, out, in_sem, out_sem):
    arrive = pltpu.make_async_copy(raw_ref, raw, in_sem)
    arrive.start()
    mean = column_mean(totals_ref)
    arrive.wait()
    rows[...] = centre(raw[...], mean)
    leave = []
    for n in range(1024 // TILE):
        at = pl.ds(n * TILE, TILE)
        out[:, at] = gram(rows[...], centred_ref[at, :]).astype(jnp.bfloat16)
        leave.append(pltpu.make_async_copy(out.at[:, at], out_ref.at[:, at], out_sem.at[n]))
        leave[-1].start()
    for copy in leave:
        copy.wait()


def fold_kernel(got_ref, result_ref, tiles_ref):
    total = jnp.sum(got_ref[...].astype(jnp.float32), axis=0)
    result_ref[...] = total.astype(jnp.bfloat16)
    for b in range(8):
        turned = total[:, b * 128 : (b + 1) * 128].T
        for p in range(2):
            tile = turned[p * 64 : (p + 1) * 64]
            tiles_ref[2 * b + p] = jnp.concatenate([tile[:32], tile[32:]], axis=1).astype(jnp.bfloat16)


def output_kernel(arrived_ref, tiles_ref, keep_ref, other_ref, place_ref, diag_ref, out_ref):
    place = place_ref[0]
    diag_ref[...] = keep_ref[...] + other_ref[...].astype(jnp.float32)
    out_ref[1 - place] = arrived_ref[...].astype(jnp.float32)
    for q in range(16):
        tile = tiles_ref[q].astype(jnp.float32)
        out_ref[place, :32, q * 64 : (q + 1) * 64] = tile[:, :64]
        out_ref[place, 32:, q * 64 : (q + 1) * 64] = tile[:, 64:]


def exchange(mask, total, jac, sister, core):
    totals = lax.all_to_all(total, SAMP, 0, 0, tiled=True)
    half = pl.pallas_call(
        half_kernel,
        out_shape=jax.ShapeDtypeStruct((512, 1024), jnp.bfloat16),
        in_specs=[pl.BlockSpec(memory_space=pltpu.VMEM)] * 2 + [pl.BlockSpec(memory_space=pltpu.SMEM)],
        cost_estimate=pl.CostEstimate(flops=0, bytes_accessed=2 << 20, transcendentals=0),
        compiler_params=pltpu.CompilerParams(vmem_limit_bytes=24 << 20),
    )(jac, sister, core)
    raw = lax.ppermute(half, SAMP, [(s, d) for d, s in enumerate(sources(mask))])
    own, partial = pl.pallas_call(
        own_kernel,
        out_shape=(
            jax.ShapeDtypeStruct((1024, 1024), jnp.bfloat16),
            jax.ShapeDtypeStruct((512, 1024), jnp.bfloat16),
        ),
        in_specs=[pl.BlockSpec(memory_space=pltpu.VMEM)] * 3 + [pl.BlockSpec(memory_space=pltpu.SMEM)],
        scratch_shapes=[pltpu.VMEM((512, 1024), jnp.bfloat16)],
        cost_estimate=pl.CostEstimate(flops=2 << 31, bytes_accessed=6 << 20, transcendentals=0),
        compiler_params=pltpu.CompilerParams(vmem_limit_bytes=24 << 20),
    )(jac, sister, totals, core)
    diag = lax.all_to_all(partial.reshape(4, 128, 1024), "x", 0, 0, tiled=True)
    return raw, own, diag, totals


def finish(mask, result):
    back = [(d, s) for d, s in enumerate(sources(mask))]
    return lax.ppermute(result, SAMP, back), parity(lax.axis_index(SAMP), mask)


def shards(jac, partners):
    first = partners[0, 0]
    core = lax.axis_index("core")
    sister = lax.ppermute(jac, "core", [(0, 1), (1, 0)])
    sums = jax.ShapeDtypeStruct((16, 8, 128), jnp.float32)
    total, index = pl.pallas_call(
        own_total_kernel,
        out_shape=(sums, jax.ShapeDtypeStruct((1,), jnp.int32)),
        in_specs=[pl.BlockSpec(memory_space=pltpu.VMEM), pl.BlockSpec(memory_space=pltpu.SMEM)],
        out_specs=(pl.BlockSpec(memory_space=pltpu.VMEM), pl.BlockSpec(memory_space=pltpu.SMEM)),
        cost_estimate=pl.CostEstimate(flops=16 << 20, bytes_accessed=1 << 20, transcendentals=0),
        compiler_params=pltpu.CompilerParams(vmem_limit_bytes=24 << 20),
    )(jac, partners)
    index = index[0]
    total = vmem_call(sister_total_kernel, sums, [], 16 << 20)(sister, total)
    raw, own, diag, totals = lax.switch(
        index,
        [functools.partial(exchange, m) for m in range(1, 8)],
        total, jac, sister, core.reshape(1),
    )
    diag = lax.optimization_barrier(diag)
    partial = pl.pallas_call(
        cross_kernel,
        out_shape=jax.ShapeDtypeStruct((512, 1024), jnp.bfloat16),
        in_specs=[pl.BlockSpec(memory_space=pl.ANY)] + [pl.BlockSpec(memory_space=pltpu.VMEM)] * 2,
        out_specs=pl.BlockSpec(memory_space=pl.ANY),
        scratch_shapes=[pltpu.VMEM((512, 1024), jnp.bfloat16)] * 3
        + [pltpu.SemaphoreType.DMA, pltpu.SemaphoreType.DMA((1024 // TILE,))],
        cost_estimate=pl.CostEstimate(flops=2 << 29, bytes_accessed=4 << 20, transcendentals=0),
        compiler_params=pltpu.CompilerParams(vmem_limit_bytes=24 << 20),
    )(raw, totals, own)
    diag = jnp.sum(diag.reshape(4, 2, 64, 1024).astype(jnp.float32), axis=0)
    y_hi = lax.axis_index("y_hi")
    keep, give = jnp.where(y_hi == 0, diag[0], diag[1]), jnp.where(y_hi == 0, diag[1], diag[0])
    other_half = lax.ppermute(give.astype(jnp.bfloat16), "y_hi", [(0, 1), (1, 0)])
    got = lax.all_to_all(partial.reshape(8, 64, 1024), CHIPS, 0, 0, tiled=True)
    result, tiles = vmem_call(
        fold_kernel,
        (
            jax.ShapeDtypeStruct((64, 1024), jnp.bfloat16),
            jax.ShapeDtypeStruct((16, 32, 128), jnp.bfloat16),
        ),
        [],
        1 << 20,
    )(got)
    turned = lax.all_to_all(tiles, PAR, 0, 0, tiled=True)
    arrived, par = lax.switch(index, [functools.partial(finish, m) for m in range(1, 8)], result)
    place = par ^ (first > 7).astype(jnp.int32)
    return pl.pallas_call(
        output_kernel,
        out_shape=(
            jax.ShapeDtypeStruct((64, 1024), jnp.float32),
            jax.ShapeDtypeStruct((2, 64, 1024), jnp.float32),
        ),
        in_specs=[pl.BlockSpec(memory_space=pltpu.VMEM)] * 4 + [pl.BlockSpec(memory_space=pltpu.SMEM)],
        compiler_params=pltpu.CompilerParams(vmem_limit_bytes=24 << 20),
    )(arrived, turned, keep, other_half, place.reshape(1))


def solution(mesh):
    fine = Mesh(mesh.devices.reshape(8, 2, 2, 4, 2), SAMP + PAR)
    return jax.shard_map(
        shards,
        mesh=fine,
        in_specs=(P(SAMP, PAR), P()),
        out_specs=(P(SAMP + PAR, None), P(None, SAMP + PAR, None)),
        check_vma=False,
    )
```

```python
import functools

import jax
import jax.numpy as jnp
from jax import lax
from jax.experimental import pallas as pl
from jax.experimental.pallas import tpu as pltpu
from jax.sharding import Mesh, PartitionSpec as P

SAMP = ("z", "y_lo")
PAR = ("y_hi", "x", "core")
CHIPS = ("y_hi", "x")
BITS = {1: (0, 1), 2: (1, 3), 3: (1, 3), 4: (2, 1), 5: (2, 1), 6: (1, 3), 7: (2, 3)}
TILE = 256


def parity(block, mask):
    s, t = BITS[mask]
    return ((block >> s) ^ (block >> t)) & 1


def sources(mask):
    return [i ^ (mask ^ 15 if parity(i, mask) else mask) for i in range(16)]


def gram(a, b):
    return lax.dot_general(a, b, (((1,), (1,)), ((), ())), preferred_element_type=jnp.float32)


def centre(x, mean):
    return (x.astype(jnp.float32) - mean).astype(jnp.bfloat16)


def vmem_call(kernel, outs, scratch, flops):
    return pl.pallas_call(
        kernel,
        out_shape=outs,
        scratch_shapes=scratch,
        cost_estimate=pl.CostEstimate(flops=flops, bytes_accessed=6 << 20, transcendentals=0),
        compiler_params=pltpu.CompilerParams(vmem_limit_bytes=24 << 20),
    )


def sums_of(ref):
    ones = jnp.ones((16, 1024), jnp.bfloat16)
    return jnp.dot(ones, ref[...], preferred_element_type=jnp.float32)


def own_total_kernel(own_ref, partners_ref, total_ref, index_ref):
    first = partners_ref[0, 0]
    index_ref[0] = jnp.minimum(first, 15 - first) - 1
    total = sums_of(own_ref)
    for r in range(4):
        total_ref[r : r + 1, :] = total[:1, r * 128 : (r + 1) * 128]
    total_ref[4:, :] = jnp.zeros((4, 128), jnp.float32)


def sister_total_kernel(sister_ref, before_ref, total_ref, before, sem):
    copy = pltpu.make_async_copy(before_ref, before, sem)
    copy.start()
    total = sums_of(sister_ref)
    copy.wait()
    total_ref[...] = jnp.broadcast_to(before[...][None], (16, 8, 128))
    for r in range(4):
        total_ref[:, 4 + r, :] = total[:, r * 128 : (r + 1) * 128]


def half_kernel(own_ref, sister_ref, core_ref, half_ref):
    core = core_ref[0]

    @pl.loop(0, 8)
    def _(c):
        at = pl.ds(pl.multiple_of(c * 64, 64), 64)
        half = pl.ds(pl.multiple_of(c * 128 + core * 64, 64), 64)
        half_ref[at, :512] = own_ref[half, :]
        half_ref[at, 512:] = sister_ref[half, :]


def column_mean(totals_ref):
    mean = jnp.sum(totals_ref[...], axis=0) * (1.0 / 16384)
    return jnp.concatenate([mean[r : r + 1] for r in range(8)], axis=1)


def own_kernel(own_ref, sister_ref, totals_ref, core_ref, centred_ref, out_ref, rows):
    mean = column_mean(totals_ref)
    core = core_ref[0]

    @pl.loop(0, 8)
    def _(c):
        at = pl.ds(pl.multiple_of(c * 128, 128), 128)
        centred_ref[at, :512] = centre(own_ref[at, :], mean[:, :512])
        centred_ref[at, 512:] = centre(sister_ref[at, :], mean[:, 512:])
        half = pl.ds(pl.multiple_of(c * 128 + core * 64, 64), 64)
        put = pl.ds(pl.multiple_of(((c & 3) * 2 + (c >> 2)) * 64, 64), 64)
        rows[put, :] = centred_ref[half, :]

    @pl.loop(0, 1024 // TILE)
    def _(n):
        at = pl.ds(pl.multiple_of(n * TILE, TILE), TILE)
        out_ref[:, at] = gram(rows[...], centred_ref[at, :]).astype(jnp.bfloat16)


def cross_kernel(raw_ref, totals_ref, centred_ref, out_ref, raw, rows, out, totals, in_sem, out_sem, mean_sem):
    first = pltpu.make_async_copy(totals_ref, totals, mean_sem)
    first.start()
    arrive = pltpu.make_async_copy(raw_ref, raw, in_sem)
    arrive.start()
    first.wait()
    mean = column_mean(totals)
    arrive.wait()
    rows[...] = centre(raw[...], mean)
    leave = []
    for n in range(1024 // TILE):
        at = pl.ds(n * TILE, TILE)
        out[:, at] = gram(rows[...], centred_ref[at, :]).astype(jnp.bfloat16)
        leave.append(pltpu.make_async_copy(out.at[:, at], out_ref.at[:, at], out_sem.at[n]))
        leave[-1].start()
    for copy in leave:
        copy.wait()


def fold_kernel(got_ref, result_ref, tiles_ref):
    total = jnp.sum(got_ref[...].astype(jnp.float32), axis=0)
    result_ref[...] = total.astype(jnp.bfloat16)
    for b in range(8):
        turned = total[:, b * 128 : (b + 1) * 128].T
        for p in range(2):
            tile = turned[p * 64 : (p + 1) * 64]
            tiles_ref[2 * b + p] = jnp.concatenate([tile[:32], tile[32:]], axis=1).astype(jnp.bfloat16)


def output_kernel(arrived_ref, tiles_ref, keep_ref, other_ref, place_ref, diag_ref, out_ref):
    place = place_ref[0]
    diag_ref[...] = keep_ref[...] + other_ref[...].astype(jnp.float32)
    out_ref[1 - place] = arrived_ref[...].astype(jnp.float32)
    for q in range(16):
        tile = tiles_ref[q].astype(jnp.float32)
        out_ref[place, :32, q * 64 : (q + 1) * 64] = tile[:, :64]
        out_ref[place, 32:, q * 64 : (q + 1) * 64] = tile[:, 64:]


def exchange(mask, total, jac, sister, core):
    totals = lax.all_to_all(total, SAMP, 0, 0, tiled=True)
    half = pl.pallas_call(
        half_kernel,
        out_shape=jax.ShapeDtypeStruct((512, 1024), jnp.bfloat16),
        in_specs=[pl.BlockSpec(memory_space=pltpu.VMEM)] * 2 + [pl.BlockSpec(memory_space=pltpu.SMEM)],
        cost_estimate=pl.CostEstimate(flops=0, bytes_accessed=2 << 20, transcendentals=0),
        compiler_params=pltpu.CompilerParams(vmem_limit_bytes=24 << 20),
    )(jac, sister, core)
    raw = lax.ppermute(half, SAMP, [(s, d) for d, s in enumerate(sources(mask))])
    own, partial = pl.pallas_call(
        own_kernel,
        out_shape=(
            jax.ShapeDtypeStruct((1024, 1024), jnp.bfloat16),
            jax.ShapeDtypeStruct((512, 1024), jnp.bfloat16),
        ),
        in_specs=[pl.BlockSpec(memory_space=pltpu.VMEM)] * 3 + [pl.BlockSpec(memory_space=pltpu.SMEM)],
        scratch_shapes=[pltpu.VMEM((512, 1024), jnp.bfloat16)],
        cost_estimate=pl.CostEstimate(flops=2 << 31, bytes_accessed=6 << 20, transcendentals=0),
        compiler_params=pltpu.CompilerParams(vmem_limit_bytes=24 << 20),
    )(jac, sister, totals, core)
    diag = lax.all_to_all(partial.reshape(4, 128, 1024), "x", 0, 0, tiled=True)
    return raw, own, diag, totals


def finish(mask, result):
    back = [(d, s) for d, s in enumerate(sources(mask))]
    return lax.ppermute(result, SAMP, back), parity(lax.axis_index(SAMP), mask)


def shards(jac, partners):
    first = partners[0, 0]
    core = lax.axis_index("core")
    sister = lax.ppermute(jac, "core", [(0, 1), (1, 0)])
    sums = jax.ShapeDtypeStruct((16, 8, 128), jnp.float32)
    total, index = pl.pallas_call(
        own_total_kernel,
        out_shape=(jax.ShapeDtypeStruct((8, 128), jnp.float32), jax.ShapeDtypeStruct((1,), jnp.int32)),
        in_specs=[pl.BlockSpec(memory_space=pltpu.VMEM), pl.BlockSpec(memory_space=pltpu.SMEM)],
        out_specs=(pl.BlockSpec(memory_space=pltpu.VMEM), pl.BlockSpec(memory_space=pltpu.SMEM)),
        cost_estimate=pl.CostEstimate(flops=16 << 20, bytes_accessed=1 << 20, transcendentals=0),
        compiler_params=pltpu.CompilerParams(vmem_limit_bytes=24 << 20),
    )(jac, partners)
    index = index[0]
    total = pl.pallas_call(
        sister_total_kernel,
        out_shape=sums,
        in_specs=[pl.BlockSpec(memory_space=pltpu.VMEM), pl.BlockSpec(memory_space=pl.ANY)],
        scratch_shapes=[pltpu.VMEM((8, 128), jnp.float32), pltpu.SemaphoreType.DMA],
        cost_estimate=pl.CostEstimate(flops=16 << 20, bytes_accessed=1 << 20, transcendentals=0),
        compiler_params=pltpu.CompilerParams(vmem_limit_bytes=24 << 20),
    )(sister, total)
    raw, own, diag, totals = lax.switch(
        index,
        [functools.partial(exchange, m) for m in range(1, 8)],
        total, jac, sister, core.reshape(1),
    )
    diag = lax.optimization_barrier(diag)
    partial = pl.pallas_call(
        cross_kernel,
        out_shape=jax.ShapeDtypeStruct((512, 1024), jnp.bfloat16),
        in_specs=[pl.BlockSpec(memory_space=pl.ANY)] * 2 + [pl.BlockSpec(memory_space=pltpu.VMEM)],
        out_specs=pl.BlockSpec(memory_space=pl.ANY),
        scratch_shapes=[pltpu.VMEM((512, 1024), jnp.bfloat16)] * 3
        + [pltpu.VMEM((16, 8, 128), jnp.float32)]
        + [pltpu.SemaphoreType.DMA, pltpu.SemaphoreType.DMA((1024 // TILE,)), pltpu.SemaphoreType.DMA],
        cost_estimate=pl.CostEstimate(flops=2 << 29, bytes_accessed=4 << 20, transcendentals=0),
        compiler_params=pltpu.CompilerParams(vmem_limit_bytes=24 << 20),
    )(raw, totals, own)
    diag = jnp.sum(diag.reshape(4, 2, 64, 1024).astype(jnp.float32), axis=0)
    y_hi = lax.axis_index("y_hi")
    keep, give = jnp.where(y_hi == 0, diag[0], diag[1]), jnp.where(y_hi == 0, diag[1], diag[0])
    other_half = lax.ppermute(give.astype(jnp.bfloat16), "y_hi", [(0, 1), (1, 0)])
    got = lax.all_to_all(partial.reshape(8, 64, 1024), CHIPS, 0, 0, tiled=True)
    result, tiles = vmem_call(
        fold_kernel,
        (
            jax.ShapeDtypeStruct((64, 1024), jnp.bfloat16),
            jax.ShapeDtypeStruct((16, 32, 128), jnp.bfloat16),
        ),
        [],
        1 << 20,
    )(got)
    turned = lax.all_to_all(tiles, PAR, 0, 0, tiled=True)
    arrived, par = lax.switch(index, [functools.partial(finish, m) for m in range(1, 8)], result)
    place = par ^ (first > 7).astype(jnp.int32)
    return pl.pallas_call(
        output_kernel,
        out_shape=(
            jax.ShapeDtypeStruct((64, 1024), jnp.float32),
            jax.ShapeDtypeStruct((2, 64, 1024), jnp.float32),
        ),
        in_specs=[pl.BlockSpec(memory_space=pltpu.VMEM)] * 4 + [pl.BlockSpec(memory_space=pltpu.SMEM)],
        compiler_params=pltpu.CompilerParams(vmem_limit_bytes=24 << 20),
    )(arrived, turned, keep, other_half, place.reshape(1))


def solution(mesh):
    fine = Mesh(mesh.devices.reshape(8, 2, 2, 4, 2), SAMP + PAR)
    return jax.shard_map(
        shards,
        mesh=fine,
        in_specs=(P(SAMP, PAR), P()),
        out_specs=(P(SAMP + PAR, None), P(None, SAMP + PAR, None)),
        check_vma=False,
    )
```

```python
import functools

import jax
import jax.numpy as jnp
from jax import lax
from jax.experimental import pallas as pl
from jax.experimental.pallas import tpu as pltpu
from jax.sharding import Mesh, PartitionSpec as P

SAMP = ("z", "y_lo")
PAR = ("y_hi", "x", "core")
CHIPS = ("y_hi", "x")
BITS = {1: (0, 1), 2: (1, 3), 3: (1, 3), 4: (2, 1), 5: (2, 1), 6: (1, 3), 7: (2, 3)}
TILE = 256
OWN_TILE = 512


def parity(block, mask):
    s, t = BITS[mask]
    return ((block >> s) ^ (block >> t)) & 1


def sources(mask):
    return [i ^ (mask ^ 15 if parity(i, mask) else mask) for i in range(16)]


def gram(a, b):
    return lax.dot_general(a, b, (((1,), (1,)), ((), ())), preferred_element_type=jnp.float32)


def centre(x, mean):
    return (x.astype(jnp.float32) - mean).astype(jnp.bfloat16)


def vmem_call(kernel, outs, scratch, flops):
    return pl.pallas_call(
        kernel,
        out_shape=outs,
        scratch_shapes=scratch,
        cost_estimate=pl.CostEstimate(flops=flops, bytes_accessed=6 << 20, transcendentals=0),
        compiler_params=pltpu.CompilerParams(vmem_limit_bytes=24 << 20),
    )


def sums_of(ref):
    ones = jnp.ones((16, 1024), jnp.bfloat16)
    return jnp.dot(ones, ref[...], preferred_element_type=jnp.float32)


def own_total_kernel(own_ref, partners_ref, total_ref, index_ref):
    first = partners_ref[0, 0]
    index_ref[0] = jnp.minimum(first, 15 - first) - 1
    total = sums_of(own_ref)
    for r in range(4):
        total_ref[r : r + 1, :] = total[:1, r * 128 : (r + 1) * 128]
    total_ref[4:, :] = jnp.zeros((4, 128), jnp.float32)


def sister_total_kernel(sister_ref, before_ref, total_ref, before, sem):
    copy = pltpu.make_async_copy(before_ref, before, sem)
    copy.start()
    total = sums_of(sister_ref)
    copy.wait()
    total_ref[...] = jnp.broadcast_to(before[...][None], (16, 8, 128))
    for r in range(4):
        total_ref[:, 4 + r, :] = total[:, r * 128 : (r + 1) * 128]


def half_kernel(own_ref, sister_ref, core_ref, half_ref):
    core = core_ref[0]

    @pl.loop(0, 8)
    def _(c):
        at = pl.ds(pl.multiple_of(c * 64, 64), 64)
        half = pl.ds(pl.multiple_of(c * 128 + core * 64, 64), 64)
        half_ref[at, :512] = own_ref[half, :]
        half_ref[at, 512:] = sister_ref[half, :]


def column_mean(totals_ref):
    mean = jnp.sum(totals_ref[...], axis=0) * (1.0 / 16384)
    return jnp.concatenate([mean[r : r + 1] for r in range(8)], axis=1)


def own_kernel(own_ref, sister_ref, totals_ref, core_ref, centred_ref, out_ref, rows):
    mean = column_mean(totals_ref)
    core = core_ref[0]

    @pl.loop(0, 8)
    def _(c):
        at = pl.ds(pl.multiple_of(c * 128, 128), 128)
        centred_ref[at, :512] = centre(own_ref[at, :], mean[:, :512])
        centred_ref[at, 512:] = centre(sister_ref[at, :], mean[:, 512:])
        half = pl.ds(pl.multiple_of(c * 128 + core * 64, 64), 64)
        put = pl.ds(pl.multiple_of(((c & 3) * 2 + (c >> 2)) * 64, 64), 64)
        rows[put, :] = centred_ref[half, :]

    @pl.loop(0, 1024 // OWN_TILE)
    def _(n):
        at = pl.ds(pl.multiple_of(n * OWN_TILE, OWN_TILE), OWN_TILE)
        out_ref[:, at] = gram(rows[...], centred_ref[at, :]).astype(jnp.bfloat16)


def cross_kernel(raw_ref, totals_ref, centred_ref, out_ref, raw, rows, out, totals, in_sem, out_sem, mean_sem):
    first = pltpu.make_async_copy(totals_ref, totals, mean_sem)
    first.start()
    parts = [pl.ds(i * 128, 128) for i in range(4)]
    arrive = [pltpu.make_async_copy(raw_ref.at[at], raw.at[at], in_sem.at[i]) for i, at in enumerate(parts)]
    for copy in arrive:
        copy.start()
    first.wait()
    mean = column_mean(totals)
    for copy, at in zip(arrive, parts):
        copy.wait()
        rows[at] = centre(raw[at], mean)
    leave = []
    for n in range(1024 // TILE):
        at = pl.ds(n * TILE, TILE)
        out[:, at] = gram(rows[...], centred_ref[at, :]).astype(jnp.bfloat16)
        leave.append(pltpu.make_async_copy(out.at[:, at], out_ref.at[:, at], out_sem.at[n]))
        leave[-1].start()
    for copy in leave:
        copy.wait()


def fold_kernel(got_ref, result_ref, tiles_ref):
    total = jnp.sum(got_ref[...].astype(jnp.float32), axis=0)
    result_ref[...] = total.astype(jnp.bfloat16)
    for b in range(8):
        turned = total[:, b * 128 : (b + 1) * 128].astype(jnp.bfloat16).T
        for p in range(2):
            tile = turned[p * 64 : (p + 1) * 64]
            tiles_ref[2 * b + p] = jnp.concatenate([tile[:32], tile[32:]], axis=1)


def output_kernel(arrived_ref, tiles_ref, keep_ref, other_ref, place_ref, diag_ref, out_ref):
    place = place_ref[0]
    diag_ref[...] = keep_ref[...] + other_ref[...].astype(jnp.float32)
    out_ref[1 - place] = arrived_ref[...].astype(jnp.float32)
    for q in range(16):
        tile = tiles_ref[q].astype(jnp.float32)
        out_ref[place, :32, q * 64 : (q + 1) * 64] = tile[:, :64]
        out_ref[place, 32:, q * 64 : (q + 1) * 64] = tile[:, 64:]


def exchange(mask, total, jac, sister, core):
    totals = lax.all_to_all(total, SAMP, 0, 0, tiled=True)
    half = pl.pallas_call(
        half_kernel,
        out_shape=jax.ShapeDtypeStruct((512, 1024), jnp.bfloat16),
        in_specs=[pl.BlockSpec(memory_space=pltpu.VMEM)] * 2 + [pl.BlockSpec(memory_space=pltpu.SMEM)],
        cost_estimate=pl.CostEstimate(flops=0, bytes_accessed=2 << 20, transcendentals=0),
        compiler_params=pltpu.CompilerParams(vmem_limit_bytes=24 << 20),
    )(jac, sister, core)
    raw = lax.ppermute(half, SAMP, [(s, d) for d, s in enumerate(sources(mask))])
    own, partial = pl.pallas_call(
        own_kernel,
        out_shape=(
            jax.ShapeDtypeStruct((1024, 1024), jnp.bfloat16),
            jax.ShapeDtypeStruct((512, 1024), jnp.bfloat16),
        ),
        in_specs=[pl.BlockSpec(memory_space=pltpu.VMEM)] * 3 + [pl.BlockSpec(memory_space=pltpu.SMEM)],
        scratch_shapes=[pltpu.VMEM((512, 1024), jnp.bfloat16)],
        cost_estimate=pl.CostEstimate(flops=2 << 31, bytes_accessed=6 << 20, transcendentals=0),
        compiler_params=pltpu.CompilerParams(vmem_limit_bytes=24 << 20),
    )(jac, sister, totals, core)
    diag = lax.all_to_all(partial.reshape(4, 128, 1024), "x", 0, 0, tiled=True)
    return raw, own, diag, totals


def finish(mask, result):
    back = [(d, s) for d, s in enumerate(sources(mask))]
    return lax.ppermute(result, SAMP, back), parity(lax.axis_index(SAMP), mask)


def shards(jac, partners):
    first = partners[0, 0]
    core = lax.axis_index("core")
    sister = lax.ppermute(jac, "core", [(0, 1), (1, 0)])
    sums = jax.ShapeDtypeStruct((16, 8, 128), jnp.float32)
    total, index = pl.pallas_call(
        own_total_kernel,
        out_shape=(jax.ShapeDtypeStruct((8, 128), jnp.float32), jax.ShapeDtypeStruct((1,), jnp.int32)),
        in_specs=[pl.BlockSpec(memory_space=pltpu.VMEM), pl.BlockSpec(memory_space=pltpu.SMEM)],
        out_specs=(pl.BlockSpec(memory_space=pltpu.VMEM), pl.BlockSpec(memory_space=pltpu.SMEM)),
        cost_estimate=pl.CostEstimate(flops=16 << 20, bytes_accessed=1 << 20, transcendentals=0),
        compiler_params=pltpu.CompilerParams(vmem_limit_bytes=24 << 20),
    )(jac, partners)
    index = index[0]
    total = pl.pallas_call(
        sister_total_kernel,
        out_shape=sums,
        in_specs=[pl.BlockSpec(memory_space=pltpu.VMEM), pl.BlockSpec(memory_space=pl.ANY)],
        scratch_shapes=[pltpu.VMEM((8, 128), jnp.float32), pltpu.SemaphoreType.DMA],
        cost_estimate=pl.CostEstimate(flops=16 << 20, bytes_accessed=1 << 20, transcendentals=0),
        compiler_params=pltpu.CompilerParams(vmem_limit_bytes=24 << 20),
    )(sister, total)
    raw, own, diag, totals = lax.switch(
        index,
        [functools.partial(exchange, m) for m in range(1, 8)],
        total, jac, sister, core.reshape(1),
    )
    diag = lax.optimization_barrier(diag)
    partial = pl.pallas_call(
        cross_kernel,
        out_shape=jax.ShapeDtypeStruct((512, 1024), jnp.bfloat16),
        in_specs=[pl.BlockSpec(memory_space=pl.ANY)] * 2 + [pl.BlockSpec(memory_space=pltpu.VMEM)],
        out_specs=pl.BlockSpec(memory_space=pl.ANY),
        scratch_shapes=[pltpu.VMEM((512, 1024), jnp.bfloat16)] * 3
        + [pltpu.VMEM((16, 8, 128), jnp.float32)]
        + [pltpu.SemaphoreType.DMA((4,)), pltpu.SemaphoreType.DMA((1024 // TILE,)), pltpu.SemaphoreType.DMA],
        cost_estimate=pl.CostEstimate(flops=2 << 29, bytes_accessed=4 << 20, transcendentals=0),
        compiler_params=pltpu.CompilerParams(vmem_limit_bytes=24 << 20),
    )(raw, totals, own)
    diag = jnp.sum(diag.reshape(4, 2, 64, 1024).astype(jnp.float32), axis=0)
    y_hi = lax.axis_index("y_hi")
    keep, give = jnp.where(y_hi == 0, diag[0], diag[1]), jnp.where(y_hi == 0, diag[1], diag[0])
    other_half = lax.ppermute(give.astype(jnp.bfloat16), "y_hi", [(0, 1), (1, 0)])
    got = lax.all_to_all(partial.reshape(8, 64, 1024), CHIPS, 0, 0, tiled=True)
    result, tiles = vmem_call(
        fold_kernel,
        (
            jax.ShapeDtypeStruct((64, 1024), jnp.bfloat16),
            jax.ShapeDtypeStruct((16, 32, 128), jnp.bfloat16),
        ),
        [],
        1 << 20,
    )(got)
    turned = lax.all_to_all(tiles, PAR, 0, 0, tiled=True)
    arrived, par = lax.switch(index, [functools.partial(finish, m) for m in range(1, 8)], result)
    place = par ^ (first > 7).astype(jnp.int32)
    return pl.pallas_call(
        output_kernel,
        out_shape=(
            jax.ShapeDtypeStruct((64, 1024), jnp.float32),
            jax.ShapeDtypeStruct((2, 64, 1024), jnp.float32),
        ),
        in_specs=[pl.BlockSpec(memory_space=pltpu.VMEM)] * 4 + [pl.BlockSpec(memory_space=pltpu.SMEM)],
        compiler_params=pltpu.CompilerParams(vmem_limit_bytes=24 << 20),
    )(arrived, turned, keep, other_half, place.reshape(1))


def solution(mesh):
    fine = Mesh(mesh.devices.reshape(8, 2, 2, 4, 2), SAMP + PAR)
    return jax.shard_map(
        shards,
        mesh=fine,
        in_specs=(P(SAMP, PAR), P()),
        out_specs=(P(SAMP + PAR, None), P(None, SAMP + PAR, None)),
        check_vma=False,
    )
```
